32 devices in a mesh: comp: 2 (over x), face: 16 (over z, y, core).
Axes of the slice: x: 2, y: 2, z: 4, core: 2. Of those that a mesh axis runs over, the one named last changes fastest.
Arguments:
- state: bfloat16 [2, 16, 4096], P('comp', None, 'face'), may hold values from -6 to 6
- cotangent: bfloat16 [2, 16, 4096], P('comp', None, 'face'), may hold values from -6 to 6
- land_sea: int32 [4096], P('face'), may hold values 0 or 1
- turn_table: int32 [16, 4], replicated, may hold values from 0 to 3
- first_kernel: bfloat16 [2, 216, 256], P('comp'), may hold values from -0.625 to 0.625
- mid_kernel: bfloat16 [2, 2304, 256], P('comp'), may hold values from -0.1875 to 0.1875
- out_kernel: bfloat16 [2, 2304, 16], P('comp'), may hold values from -0.1875 to 0.1875
- first_gates: int32 [2, 216, 64], P('comp'), may hold values from 0 to 5
- mid_gates: int32 [2, 2304, 64], P('comp'), may hold values from 0 to 5
- out_gates: int32 [2, 2304, 4], P('comp'), may hold values from 0 to 5
Outputs:
- upcoming_climate_estimate: bfloat16 [2, 16, 4096], P('comp', None, 'face')
- condition_adjoint_grid: float32 [2, 16, 4096], P('comp', None, 'face')
- opening_filter_adjoint: float32 [2, 216, 256], P('comp')
- central_filter_adjoint: float32 [2, 589824], P('comp', 'face')
- closing_filter_adjoint: float32 [2, 36864], P('comp', 'face')
The draws below stay inside these ranges and needn't reach their ends.
Inputs may be any that keep to these rules, and one draw needn't show every extreme that they name: `mid_gates`: a gate value picks one of the six ways of keeping 2 of 4 consecutive output channels. `first_gates`: a gate value picks one of the six ways of keeping 2 of 4 consecutive output channels. `out_gates`: a gate value picks one of the six ways of keeping 2 of 4 consecutive output channels.
All inputs are finite; a program needn't handle non-finite values. No bound on the sum of `land_sea` on one device may be relied on, other than what follows from the above.
Results may differ from the reference program's by a relative error of at most 0.0052.
Values may be sent and summed in bfloat16 or wider, within the bound.
A program may use at most 64 MiB of HBM per device.

```python
from functools import partial
import jax
import jax.numpy as jnp
from jax import lax

FIELDS = 16
COUPLED = 8
HIDDEN_SIZE = 256
ROW_TILES = 4
TS = 16
IN_CH = 24
CELLS = 256
TILES = 16


def touch_ends(result, key, smallest, largest):
    index_at = [jax.random.randint(jax.random.fold_in(key, axis), (), 0, length) for axis, length in enumerate(result.shape)]
    longest = result.shape.index(max(result.shape))
    neighbour = index_at[:longest] + [(index_at[longest] + 1) % result.shape[longest]] + index_at[longest + 1:]
    return result.at[tuple(index_at)].set(smallest).at[tuple(neighbour)].set(largest)


def block_levels(key, dims, pieces, low, high):
    factor_of = 1.0
    for axis_at, blocks in pieces:
        heights = jax.random.uniform(jax.random.fold_in(jax.random.fold_in(key, 6), axis_at), (blocks,), jnp.float32, low / len(pieces), high / len(pieces))
        factor_of = factor_of * jnp.repeat(jnp.exp(heights), dims[axis_at] // blocks).reshape((-1,) + (1,) * (len(dims) - 1 - axis_at))
    return factor_of


def gaussian(key, shape, scale, most, pieces=(), kind=jnp.bfloat16):
    values = jax.random.normal(key, shape, jnp.float32) * scale
    if len(pieces) > 0:
        values = block_levels(key, shape, pieces, -0.22, 0.18) * values
    return jnp.clip(values, min=-most, max=most).astype(kind)


def setup_inputs(seed: int = 0) -> dict:
    streams_of = jax.random.split(jax.random.key(seed), 11)
    return {
        "state": gaussian(streams_of[0], (2, FIELDS, TILES * CELLS), 1.0, 6.0, ((0, 2), (2, 16))),
        "cotangent": gaussian(streams_of[1], (2, FIELDS, TILES * CELLS), 1.0, 6.0, ((0, 2), (2, 16))),
        "land_sea": touch_ends((jax.random.randint(streams_of[2], (TILES * CELLS,), 0, 3) < 2).astype(jnp.int32), jax.random.fold_in(streams_of[2], 1), 0, 1),
        "turn_table": touch_ends(jax.random.randint(streams_of[3], (TILES, 4), 0, 4), jax.random.fold_in(streams_of[3], 1), 0, 3).astype(jnp.int32),
        "first_kernel": gaussian(streams_of[4], (2, 9 * IN_CH, HIDDEN_SIZE), (9 * IN_CH // 2) ** -0.5, 0.625, ((0, 2),)),
        "mid_kernel": gaussian(streams_of[5], (2, 9 * HIDDEN_SIZE, HIDDEN_SIZE), (9 * HIDDEN_SIZE // 2) ** -0.5, 0.1875, ((0, 2),)),
        "out_kernel": gaussian(streams_of[6], (2, 9 * HIDDEN_SIZE, FIELDS), (9 * HIDDEN_SIZE // 2) ** -0.5, 0.1875, ((0, 2),)),
        "first_gates": touch_ends(jax.random.randint(streams_of[7], (2, 9 * IN_CH, HIDDEN_SIZE // 4), 0, 6), jax.random.fold_in(streams_of[7], 1), 0, 5).astype(jnp.int32),
        "mid_gates": touch_ends(jax.random.randint(streams_of[8], (2, 9 * HIDDEN_SIZE, HIDDEN_SIZE // 4), 0, 6), jax.random.fold_in(streams_of[8], 1), 0, 5).astype(jnp.int32),
        "out_gates": touch_ends(jax.random.randint(streams_of[9], (2, 9 * HIDDEN_SIZE, FIELDS // 4), 0, 6), jax.random.fold_in(streams_of[9], 1), 0, 5).astype(jnp.int32),
    }


def gate_pair(gates):
    low = (gates >= 3).astype(jnp.int32) + (gates >= 5).astype(jnp.int32)
    high = jnp.where(gates == 0, 1, jnp.where((gates == 1) | (gates == 3), 2, 3)).astype(jnp.int32)
    return (low, high)

def gate_keep(gates):
    low, high = gate_pair(gates)
    lanes = jnp.arange(4, dtype=jnp.int32)
    keep = (low[..., None] == lanes) | (high[..., None] == lanes)
    return keep.reshape(gates.shape[0], gates.shape[1] * 4)

def edge_of(square, side):
    if side == 0:
        return square[:, :, -1]
    if side == 1:
        return square[:, :, 0]
    if side == 2:
        return square[:, -1, :]
    return square[:, 0, :]

def turned_edge(square, turns, side):
    return edge_of(jnp.rot90(square, turns, axes=(1, 2)), side)

def take_edge(square, turn, side):
    return lax.switch(turn, [partial(turned_edge, turns=j, side=side) for j in range(4)], square)

def pad_all(tiles, turn_table):
    shifts = (1, -1, ROW_TILES, -ROW_TILES)
    strips = [jax.vmap(partial(take_edge, side=side))(jnp.roll(tiles, shifts[side], 0), turn_table[:, side]) for side in range(4)]
    padded = jnp.pad(tiles, ((0, 0), (0, 0), (1, 1), (1, 1)))
    padded = padded.at[:, :, 1:-1, 0].set(strips[0])
    padded = padded.at[:, :, 1:-1, -1].set(strips[1])
    padded = padded.at[:, :, 0, 1:-1].set(strips[2])
    padded = padded.at[:, :, -1, 1:-1].set(strips[3])
    return padded

def unfold(padded, breadth_count):
    feature_depth = padded.shape[0]
    return jnp.concatenate([padded[:, vertical_place:vertical_place + breadth_count, horizontal_place:horizontal_place + breadth_count].reshape(feature_depth, breadth_count * breadth_count) for vertical_place in range(3) for horizontal_place in range(3)], 0)

def fold(columns, feature_depth, breadth_count):
    prognosis_outcome = jnp.zeros((feature_depth, breadth_count + 2, breadth_count + 2), jnp.float32)
    index = 0
    for vertical_place in range(3):
        for horizontal_place in range(3):
            square_piece = columns[index * feature_depth:(index + 1) * feature_depth].reshape(feature_depth, breadth_count, breadth_count)
            prognosis_outcome = prognosis_outcome.at[:, vertical_place:vertical_place + breadth_count, horizontal_place:horizontal_place + breadth_count].add(square_piece)
            index = index + 1
    return prognosis_outcome

def correlate_everything(padded, kernel):

    def one_tile(square):
        return lax.dot_general(kernel, unfold(square, TS), (((0,), (0,)), ((), ())), preferred_element_type=jnp.float32)
    return lax.map(one_tile, padded)

def back_all(padded, grads, kernel):
    feature_depth = padded.shape[1]

    def step(total, pair):
        square, grad = pair
        columns = unfold(square, TS)
        total = total + lax.dot_general(columns, grad, (((1,), (1,)), ((), ())), preferred_element_type=jnp.float32)
        back = jnp.dot(kernel, grad, preferred_element_type=jnp.float32)
        return (total, fold(back, feature_depth, TS))
    start = jnp.zeros((kernel.shape[0], kernel.shape[1]), jnp.float32)
    return lax.scan(step, start, (padded, grads))

def slope(values):
    sig = jax.nn.sigmoid(values)
    return sig * (1.0 + values * (1.0 - sig))

def reference(state, cotangent, land_sea, turn_table, first_kernel, mid_kernel, out_kernel, first_gates, mid_gates, out_gates):
    cells = TS * TS
    sea = land_sea.astype(jnp.float32).reshape(TILES, 1, cells)

    def as_tiles(flat):
        feature_depth = flat.shape[0]
        return flat.reshape(feature_depth, TILES, cells).transpose(1, 0, 2)

    def linear_layout(tiles):
        return tiles.transpose(1, 0, 2).reshape(tiles.shape[1], TILES * cells)

    def squares(tiles):
        return tiles.reshape(TILES, tiles.shape[1], TS, TS)

    def unpad(dpad):
        zero_tiles = jnp.zeros((TILES, dpad.shape[1], TS, TS), jnp.float32)
        _, pull = jax.vjp(lambda tiles: pad_all(tiles, turn_table), zero_tiles)
        return pull(dpad)[0].reshape(TILES, dpad.shape[1], cells)

    def component(comp):
        local_region_quantity = state[comp]
        partner = state[1 - comp][:COUPLED]
        inputs = jnp.concatenate([local_region_quantity, partner], 0)
        opening_keep = gate_keep(first_gates[comp])
        central_keep = gate_keep(mid_gates[comp])
        closing_keep = gate_keep(out_gates[comp])
        kernel_first = jnp.where(opening_keep, first_kernel[comp], jnp.zeros((), jnp.bfloat16))
        kernel_mid = jnp.where(central_keep, mid_kernel[comp], jnp.zeros((), jnp.bfloat16))
        stencil_produced = jnp.where(closing_keep, out_kernel[comp], jnp.zeros((), jnp.bfloat16))
        pad_zero = pad_all(squares(as_tiles(inputs)), turn_table)
        act_one = correlate_everything(pad_zero, kernel_first)
        hid_one = jax.nn.silu(act_one).astype(jnp.bfloat16)
        pad_one = pad_all(squares(hid_one), turn_table)
        act_two = correlate_everything(pad_one, kernel_mid)
        hid_two = jax.nn.silu(act_two).astype(jnp.bfloat16)
        border_fill_two = pad_all(squares(hid_two), turn_table)
        prognosis_outcome = correlate_everything(border_fill_two, stencil_produced)
        if comp == 1:
            scaling_ratio = sea
        else:
            scaling_ratio = jnp.ones_like(sea)
        local_face_stripes = as_tiles(local_region_quantity)
        upcoming_climate_estimate = (local_face_stripes.astype(jnp.float32) + scaling_ratio * prognosis_outcome).astype(jnp.bfloat16)
        cot_tiles = as_tiles(cotangent[comp]).astype(jnp.float32)
        grad_three = (scaling_ratio * cot_tiles).astype(jnp.bfloat16)
        closing_accumulated, dpad_two = back_all(border_fill_two, grad_three, stencil_produced)
        grad_hid_two = unpad(dpad_two)
        grad_two = (grad_hid_two * slope(act_two)).astype(jnp.bfloat16)
        central_accumulated, dpad_one = back_all(pad_one, grad_two, kernel_mid)
        grad_hid_one = unpad(dpad_one)
        grad_one = (grad_hid_one * slope(act_one)).astype(jnp.bfloat16)
        opening_accumulated, dpad_zero = back_all(pad_zero, grad_one, kernel_first)
        grad_inputs = unpad(dpad_zero)
        own_domain_adjoint = cot_tiles + grad_inputs[:, :FIELDS]
        partner_domain_adjoint = grad_inputs[:, FIELDS:]
        zero_float = jnp.zeros((), jnp.float32)
        return (linear_layout(upcoming_climate_estimate), own_domain_adjoint, partner_domain_adjoint, jnp.where(opening_keep, opening_accumulated, zero_float), jnp.where(central_keep, central_accumulated, zero_float), jnp.where(closing_keep, closing_accumulated, zero_float))
    air_component_slice = component(0)
    marine_component_slice = component(1)
    atmos_grad = air_component_slice[1].at[:, :COUPLED].add(marine_component_slice[2])
    ocean_grad = marine_component_slice[1].at[:, :COUPLED].add(air_component_slice[2])
    upcoming_climate_estimate = jnp.stack([air_component_slice[0], marine_component_slice[0]], 0)
    condition_adjoint_grid = jnp.stack([linear_layout(atmos_grad), linear_layout(ocean_grad)], 0)
    opening_filter_adjoint = jnp.stack([air_component_slice[3], marine_component_slice[3]], 0)
    central_filter_adjoint = jnp.stack([air_component_slice[4].reshape(-1), marine_component_slice[4].reshape(-1)], 0)
    closing_filter_adjoint = jnp.stack([air_component_slice[5].reshape(-1), marine_component_slice[5].reshape(-1)], 0)
    return (upcoming_climate_estimate, condition_adjoint_grid, opening_filter_adjoint, central_filter_adjoint, closing_filter_adjoint)
```

```python
import functools

import jax
import jax.numpy as jnp
from jax import lax
from jax.experimental import pallas as pl
from jax.experimental.pallas import tpu as pltpu
from jax.sharding import PartitionSpec as P

FIELDS = 16
COUPLED = 8
ROW_TILES = 4
TS = 16
CELLS = TS * TS
STRIPS = 4 * TS
PADDED = 32
BF = jnp.bfloat16
F32 = jnp.float32

EDGE_MAP = (
    ((0, False), (2, True), (1, True), (3, False)),
    ((1, False), (3, True), (0, True), (2, False)),
    ((2, False), (1, False), (3, True), (0, True)),
    ((3, False), (0, False), (2, True), (1, True)),
)


def nn(x, y):
    return jnp.dot(x, y, preferred_element_type=F32)


def nt(x, y):
    return lax.dot_general(x, y, (((1,), (1,)), ((), ())), preferred_element_type=F32)


def tn(x, y):
    return lax.dot_general(x, y, (((0,), (0,)), ((), ())), preferred_element_type=F32)


def iota(shape, axis):
    return lax.broadcasted_iota(jnp.int32, shape, axis)


def split_low_high(gate, place):
    low = jnp.where(gate >= 5.0, 2.0, jnp.where(gate >= 3.0, 1.0, 0.0))
    high = jnp.where(gate == 0.0, 1.0, jnp.where((gate == 1.0) | (gate == 3.0), 2.0, 3.0))
    return jnp.where(low == place, 1.0, 0.0), jnp.where(high == place, 1.0, 0.0)


def silu_slope(v):
    sig = 1.0 / (1.0 + jnp.exp(-v))
    return v * sig, sig * (1.0 + v * (1.0 - sig))


def bit_order(count):
    bits = count.bit_length() - 1
    order = list(range(min(2, bits))) + list(range(bits - 1, 1, -1))
    pieces = []
    for slot in range(count):
        piece = 0
        for step, bit in enumerate(order):
            piece |= (slot >> (bits - 1 - step) & 1) << bit
        pieces.append(piece)
    return order, pieces


def kernel(
    count,
    turn,
    state,
    cot,
    sea,
    w1,
    w2_hbm,
    w3,
    gates1,
    gates2_hbm,
    gates3,
    up_out,
    adj_out,
    d1_out,
    d2_out,
    d3_out,
    w2,
    gates2,
    w2t,
    low2,
    high2,
    cols1,
    cols2,
    shift,
    acts,
    dh,
    w1m,
    w1pad,
    w1p,
    low1,
    high1,
    mask3,
    e0_send,
    e0_own,
    e0_partner,
    e0_inner,
    e1_send,
    e1_recv,
    h2_send,
    h2_recv,
    b2_send,
    b2_recv,
    b1_send,
    b1_recv,
    b0_send,
    b0_own,
    b0_partner,
    b0_inner_send,
    b0_inner,
    big,
    big_send,
    big_recv,
    small,
    small_send,
    small_recv,
    gathered,
    send_sem,
    recv_sem,
    load_sem,
):
    order, pieces = bit_order(count)
    steps = len(order)
    taps = w2.shape[0]
    rows = taps // count
    piece_rows = big.shape[1]
    comp = lax.axis_index("comp")
    me = lax.axis_index("face")
    other = 1 - comp
    used = [0]

    def copy_to(src, dst, component, face):
        index = used[0]
        used[0] += 1
        copy = pltpu.make_async_remote_copy(
            src_ref=src,
            dst_ref=dst,
            send_sem=send_sem.at[index],
            recv_sem=recv_sem.at[index],
            device_id=(component, face),
            device_id_type=pl.DeviceIdType.MESH,
        )
        copy.start()
        return copy

    def face_at(offset):
        return lax.rem(me + offset + count, count)

    forward = [face_at(1), face_at(-1), face_at(ROW_TILES), face_at(-ROW_TILES)]
    backward = [forward[1], forward[0], forward[3], forward[2]]
    mates = []
    for bit in order:
        mine = lax.rem(me // (1 << bit), 2)
        mates.append((mine, me + (1 - 2 * mine) * (1 << bit)))

    load_w2 = pltpu.make_async_copy(w2_hbm, w2, load_sem.at[0])
    load_g2 = pltpu.make_async_copy(gates2_hbm, gates2, load_sem.at[1])
    load_w2.start()
    load_g2.start()

    barrier = pltpu.get_barrier_semaphore()
    signals = 0
    targets = [(other, me)]
    targets += [(c, f) for c in (comp, other) for f in forward]
    targets += [(comp, mate) for _, mate in mates]
    for target in targets:
        pl.semaphore_signal(barrier, inc=1, device_id=target, device_id_type=pl.DeviceIdType.MESH)
        signals += 1

    strip = iota((STRIPS, 1), 0)
    side = strip // TS
    along = lax.rem(strip, TS)
    offsets = (1, -1, ROW_TILES, -ROW_TILES)
    edge_cell = jnp.zeros((STRIPS, 1), jnp.int32)
    for s in range(4):
        turns = turn[s, face_at(offsets[s])]
        for k in range(4):
            slot, flip = EDGE_MAP[s][k]
            j = TS - 1 - along if flip else along
            cell = (j * TS + TS - 1, j * TS, (TS - 1) * TS + j, j)[slot]
            edge_cell = jnp.where((side == s) & (turns == k), cell, edge_cell)
    pick = jnp.where(iota((STRIPS, CELLS), 1) == edge_cell, 1.0, 0.0).astype(BF)

    state_f = state[...].astype(F32)
    wide = jnp.concatenate([state_f, jnp.zeros((128 - FIELDS, CELLS), F32)], 0).astype(BF)
    e0_send[...] = nt(pick, wide).astype(BF)

    pl.semaphore_wait(barrier, signals)
    waits0 = [copy_to(state, e0_inner, other, me)]
    for component, landing in ((comp, e0_own), (other, e0_partner)):
        for s in range(4):
            part = pl.ds(s * TS, TS)
            waits0.append(copy_to(e0_send.at[part], landing.at[part], component, forward[s]))

    cell = iota((1, CELLS), 1)
    row, column = cell // TS, lax.rem(cell, TS)
    source = iota((CELLS + STRIPS, CELLS), 0)
    for a in range(3):
        for b in range(3):
            r, q = row + (a - 1), column + (b - 1)
            r_in, q_in = (r >= 0) & (r < TS), (q >= 0) & (q < TS)
            at = jnp.where(r_in & q_in, r * TS + q, -1)
            at = jnp.where(r_in & (q < 0), CELLS + r, at)
            at = jnp.where(r_in & (q >= TS), CELLS + TS + r, at)
            at = jnp.where(q_in & (r < 0), CELLS + 2 * TS + q, at)
            at = jnp.where(q_in & (r >= TS), CELLS + 3 * TS + q, at)
            shift[3 * a + b] = jnp.where(source == at, 1.0, 0.0).astype(BF)

    scale = jnp.where(comp == 1, sea[...].astype(F32), 1.0)
    cot_f = cot[...].astype(F32)
    g3 = (scale * cot_f).astype(BF)
    channel = iota((FIELDS, gates3.shape[1]), 0)
    gate3 = gates3[...].astype(F32)
    group = channel // 4
    gate_rows = jnp.where(
        group == 0,
        gate3[0:1],
        jnp.where(group == 1, gate3[1:2], jnp.where(group == 2, gate3[2:3], gate3[3:4])),
    )
    low3, high3 = split_low_high(gate_rows, lax.rem(channel, 4).astype(F32))
    keep3 = low3 + high3
    w3m = jnp.where(keep3 > 0.0, w3[...].astype(F32), 0.0).astype(BF)
    hidden = w1.shape[1]

    def tap(k):
        return slice(k * hidden, (k + 1) * hidden)

    strips_two = jnp.zeros((STRIPS, hidden), F32)
    for k in range(9):
        edge_grad = nt(shift[k, CELLS:, :], g3).astype(BF)
        strips_two += nn(edge_grad, w3m[:, tap(k)])
    b2_send[...] = strips_two.astype(BF)
    waits_b2 = []
    for s in range(4):
        part = pl.ds(s * TS, TS)
        waits_b2.append(copy_to(b2_send.at[part], b2_recv.at[part], comp, backward[s]))

    place = lax.rem(iota((1, hidden), 1), 4).astype(F32)
    spread = jnp.where(iota((hidden // 4, hidden), 0) == iota((hidden // 4, hidden), 1) // 4, 1.0, 0.0)
    spread = spread.astype(BF)
    rows_one = w1.shape[0]
    channels = rows_one // 9
    gate_one = tn(gates1[...].astype(F32).astype(BF), spread)
    lo, hi = split_low_high(gate_one, place)
    low1[...] = jnp.zeros_like(low1)
    high1[...] = jnp.zeros_like(high1)
    low1[pl.ds(0, rows_one)] = lo
    high1[pl.ds(0, rows_one)] = hi
    w1m[...] = jnp.where(lo + hi > 0.0, w1[...].astype(F32), 0.0)
    w1pad[...] = jnp.zeros_like(w1pad)
    for k in range(9):
        w1pad[pl.ds(k * PADDED, channels)] = w1m[pl.ds(k * channels, channels)]
    w1p[...] = w1pad[...].astype(BF)
    w1t = w1pad[...].T.astype(BF)

    load_w2.wait()
    load_g2.wait()
    if not rows % TS == 0:
        for ref in (low2, high2, cols1):
            ref[pl.ds(taps, 2 * TS)] = jnp.zeros((2 * TS, hidden), BF)
    for k in range(9):
        part = pl.ds(k * hidden, hidden)
        gate = tn(gates2[:, tap(k)].astype(F32).astype(BF), spread)
        lo, hi = split_low_high(gate, place)
        low2[part] = lo.astype(BF)
        high2[part] = hi.astype(BF)
        masked = jnp.where(lo + hi > 0.0, w2[part].astype(F32), 0.0)
        w2[part] = masked.astype(BF)
        w2t[:, tap(k)] = masked.T.astype(BF)

    def flipped(k):
        return shift[8 - k, :CELLS, :]

    for copy in waits0:
        copy.wait()
    inner = jnp.concatenate(
        [state_f, e0_inner[...].astype(F32)[:COUPLED], jnp.zeros((PADDED - FIELDS - COUPLED, CELLS), F32)], 0
    )
    own_t = e0_own[...].astype(F32).T
    partner_t = e0_partner[...].astype(F32).T
    halo = jnp.concatenate(
        [own_t[:FIELDS], partner_t[:COUPLED], jnp.zeros((PADDED - FIELDS - COUPLED, STRIPS), F32)], 0
    )
    field = jnp.concatenate([inner, halo], 1).astype(BF)
    cols0 = jnp.concatenate([nn(field, shift[k]) for k in range(9)], 0).astype(BF)
    act_one = nn(w1t, cols0)
    hid, slope_one = silu_slope(act_one)
    acts[...] = slope_one
    hid = hid.astype(BF)
    e1_send[...] = nt(pick, hid).astype(BF)
    waits1 = []
    for s in range(4):
        part = pl.ds(s * TS, TS)
        waits1.append(copy_to(e1_send.at[part], e1_recv.at[part], comp, forward[s]))

    for k in range(9):
        cols1[pl.ds(k * hidden, hidden)] = nn(hid, shift[k, :CELLS, :]).astype(BF)
    shifted3 = jnp.concatenate([nn(g3, flipped(k)) for k in range(9)], 0).astype(BF)
    stacked3 = jnp.concatenate([w3m[:, tap(k)] for k in range(9)], 0)
    dh[...] = tn(stacked3, shifted3)
    for copy in waits_b2:
        copy.wait()
    dh[...] += tn(b2_recv[...], pick)

    for copy in waits1:
        copy.wait()
    halo_t = e1_recv[...].astype(F32).T.astype(BF)
    for k in range(9):
        part = pl.ds(k * hidden, hidden)
        cols1[part] = cols1[part] + nn(halo_t, shift[k, CELLS:, :]).astype(BF)
    act_two = nn(w2t[...], cols1[pl.ds(0, taps)])
    hid, slope_two = silu_slope(act_two)
    g2 = (dh[...] * slope_two).astype(BF)
    hid = hid.astype(BF)

    strips_one = jnp.zeros((STRIPS, hidden), F32)
    for k in range(9):
        edge_grad = nt(shift[k, CELLS:, :], g2).astype(BF)
        strips_one += nt(edge_grad, w2[pl.ds(k * hidden, hidden)])
    b1_send[...] = strips_one.astype(BF)
    h2_send[...] = nt(pick, hid).astype(BF)
    waits_b1, waits_h2 = [], []
    for s in range(4):
        part = pl.ds(s * TS, TS)
        waits_b1.append(copy_to(b1_send.at[part], b1_recv.at[part], comp, backward[s]))
    for s in range(4):
        part = pl.ds(s * TS, TS)
        waits_h2.append(copy_to(h2_send.at[part], h2_recv.at[part], comp, forward[s]))

    lane, packed = iota((hidden, hidden // 2), 0) // 4, iota((hidden, hidden // 2), 1)
    pack_low = jnp.where(lane == packed, 1.0, 0.0).astype(BF)
    pack_high = jnp.where(lane + hidden // 4 == packed, 1.0, 0.0).astype(BF)

    def pack(term, low, high):
        return nn(term * low, pack_low) + nn(term * high, pack_high)

    def unpack(total, low, high):
        top = total.astype(BF)
        rest = (total - top.astype(F32)).astype(BF)
        return (nt(top, pack_low) + nt(rest, pack_low)) * low + (nt(top, pack_high) + nt(rest, pack_high)) * high

    aligned = rows % TS == 0
    slab = rows if aligned else piece_rows + TS

    def piece_part(index):
        return pl.ds(pl.multiple_of(index * rows // TS * TS, TS), slab)

    def settle(values, index):
        if aligned:
            return values
        return pltpu.roll(values, lax.rem(slab - lax.rem(index * rows, TS), slab), 0)[:piece_rows]

    def piece_term(index):
        part = piece_part(index)
        return settle(pack(nt(cols1[part], g2).astype(BF), low2[part], high2[part]), index)

    half = count // 2
    core = mates[0][0]
    for i in range(half):
        big_send[i] = piece_term(pieces[i] + (1 - core)).astype(BF)
    starts = [jnp.int32(0)]
    sent_at = [0]
    big_copies = [copy_to(big_send.at[pl.ds(0, half)], big_recv.at[pl.ds(0, half)], comp, mates[0][1])]
    for i in range(half):
        big[i] = piece_term(pieces[i] + core)

    total = jnp.zeros((hidden, CELLS), F32)
    for k in range(9):
        moved = nn(g2, flipped(k)).astype(BF)
        total += nn(w2[pl.ds(k * hidden, hidden)], moved)
    for copy in waits_b1:
        copy.wait()
    total += tn(b1_recv[...], pick)
    g1 = (total * acts[...]).astype(BF)

    back = nn(w1p[...], g1)
    back_zero = jnp.zeros((2 * PADDED, CELLS + STRIPS), F32)
    for k in range(9):
        piece = back[k * PADDED : (k + 1) * PADDED]
        top = piece.astype(BF)
        rest = (piece - top.astype(F32)).astype(BF)
        back_zero += nt(jnp.concatenate([top, rest], 0), shift[k])
    back_zero = back_zero[:PADDED] + back_zero[PADDED:]
    strips_zero = jnp.concatenate([back_zero[:, CELLS:], jnp.zeros((128 - PADDED, STRIPS), F32)], 0).T
    b0_send[...] = strips_zero.astype(BF)
    b0_inner_send[...] = back_zero[FIELDS : FIELDS + COUPLED, :CELLS]
    waits_b0 = [copy_to(b0_inner_send, b0_inner, other, me)]
    for component, landing in ((comp, b0_own), (other, b0_partner)):
        for s in range(4):
            part = pl.ds(s * TS, TS)
            waits_b0.append(copy_to(b0_send.at[part], landing.at[part], component, backward[s]))

    def fold_in(step, copy, held, landing):
        size = count >> (step + 1)
        offset = sum(count >> (s + 1) for s in range(step))
        copy.wait()
        for i in range(size):
            held[i] = held[i] + landing[offset + i].astype(F32)

    def pass_on(step, held, outgoing, landing):
        size = count >> (step + 1)
        offset = sum(count >> (s + 1) for s in range(step))
        mine, mate = mates[step]
        for i in range(size):
            gives = held[(1 - mine) * size + i]
            keeps = held[mine * size + i]
            outgoing[offset + i] = gives.astype(BF)
            held[i] = keeps
        return copy_to(
            outgoing.at[pl.ds(offset, size)], landing.at[pl.ds(offset, size)], comp, mate
        )

    big_copy = big_copies[0]
    fold_in(0, big_copy, big, big_recv)
    if steps > 1:
        big_copy = pass_on(1, big, big_send, big_recv)

    for copy in waits_h2:
        copy.wait()
    field = jnp.concatenate([hid, h2_recv[...].astype(F32).T.astype(BF)], 1)
    for k in range(9):
        cols2[pl.ds(k * hidden, hidden)] = nn(field, shift[k]).astype(BF)
    result = nn(w3m, cols2[...])
    up_out[...] = (state_f + scale * result).astype(BF)

    term_one = nt(cols0, g1)
    w1pad[...] = term_one
    w1m_rows = [w1pad[pl.ds(k * PADDED, channels)] for k in range(9)]
    w1m_rows.append(jnp.zeros((small.shape[0] * TS - rows_one, hidden), F32))
    term_one = jnp.concatenate(w1m_rows, 0).astype(BF)
    packed_one = pack(term_one, low1[...].astype(BF), high1[...].astype(BF))
    wide3 = small.shape[2] - hidden // 2
    for slot in range(count):
        index = pieces[slot]
        part3 = nt(g3, cols2[pl.ds(index * rows, rows)])
        mask3[index, :, pl.ds(0, rows)] = keep3[:, index * rows : (index + 1) * rows]
        small[slot, :, pl.ds(0, rows)] = part3
        small[slot, :, pl.ds(rows, wide3 - rows)] = jnp.zeros((FIELDS, wide3 - rows), F32)
        small[slot, :, pl.ds(wide3, hidden // 2)] = packed_one[index * TS : (index + 1) * TS]
    small_copy = pass_on(0, small, small_send, small_recv)

    for step in range(steps):
        if step > 0:
            fold_in(step, big_copy, big, big_recv)
            if step + 1 < steps:
                big_copy = pass_on(step + 1, big, big_send, big_recv)
        fold_in(step, small_copy, small, small_recv)
        if step + 1 < steps:
            small_copy = pass_on(step + 1, small, small_send, small_recv)

    my_slot = jnp.int32(0)
    for step in range(steps):
        my_slot = my_slot + mates[step][0] * (count >> (step + 1))
    gathered[my_slot] = small[0, :, pl.ds(wide3, hidden // 2)]
    d3_out[...] = small[0, :, pl.ds(0, rows)] * mask3[me, :, pl.ds(0, rows)]
    part = piece_part(me)
    low_mine, high_mine = (settle(ref[part].astype(F32), me) for ref in (low2, high2))
    d2_out[...] = unpack(big[0], low_mine, high_mine)
    start = my_slot
    for step in range(steps - 1, -1, -1):
        size = count >> (step + 1)
        mine, mate = mates[step]
        part = pl.ds(start, size)
        copy = copy_to(gathered.at[part], gathered.at[part], comp, mate)
        if step == steps - 1:
            for waiting in waits_b0:
                waiting.wait()
            returned = tn(b0_own[...], pick)
            coupled = tn(b0_partner[...], pick)
            own = cot_f + back_zero[:FIELDS, :CELLS] + returned[:FIELDS]
            top = own[:COUPLED] + b0_inner[...] + coupled[FIELDS : FIELDS + COUPLED]
            adj_out[...] = jnp.concatenate([top, own[COUPLED:]], 0)
        copy.wait()
        start = start - mine * size
    slot_of = [pieces.index(index) for index in range(count)]
    summed = jnp.concatenate([gathered[slot_of[i]] for i in range(-(-rows_one // TS))], 0)
    kept = summed.shape[0]
    whole = unpack(summed, low1[pl.ds(0, kept)], high1[pl.ds(0, kept)])
    d1_out[...] = whole[:rows_one]


def body(count, state, cotangent, land_sea, turn_table, w1, w2, w3, gates1, gates2, gates3):
    hidden = w1.shape[2]
    taps = w2.shape[1]
    rows = taps // count
    piece_rows = -(-rows // TS) * TS
    spare = taps if rows % TS == 0 else taps + 2 * TS
    wide3 = -(-rows // 128) * 128
    one_rows = max(count * TS, 256)
    vmem = pl.BlockSpec(memory_space=pltpu.VMEM)
    any_space = pl.BlockSpec(memory_space=pl.ANY)
    smem = pl.BlockSpec(memory_space=pltpu.SMEM)
    steps = count.bit_length() - 1
    copies = 9 + 4 + 4 + 4 + 4 + 9 + 3 * steps

    def half(*shape):
        return pltpu.VMEM(shape, BF)

    def full(*shape):
        return pltpu.VMEM(shape, F32)

    up, adj, d1, d2, d3 = pl.pallas_call(
        functools.partial(kernel, count),
        out_shape=(
            jax.ShapeDtypeStruct((FIELDS, CELLS), BF),
            jax.ShapeDtypeStruct((FIELDS, CELLS), F32),
            jax.ShapeDtypeStruct((w1.shape[1], hidden), F32),
            jax.ShapeDtypeStruct((piece_rows, hidden), F32),
            jax.ShapeDtypeStruct((FIELDS, rows), F32),
        ),
        in_specs=[smem, vmem, vmem, vmem, vmem, any_space, vmem, vmem, any_space, vmem],
        out_specs=(vmem,) * 5,
        scratch_shapes=[
            half(taps, hidden),
            pltpu.VMEM((hidden // 4, taps), jnp.int32),
            half(hidden, taps),
            half(spare, hidden),
            half(spare, hidden),
            half(spare, hidden),
            half(taps, hidden),
            half(9, CELLS + STRIPS, CELLS),
            full(hidden, CELLS),
            full(hidden, CELLS),
            full(w1.shape[1], hidden),
            full(9 * PADDED, hidden),
            half(9 * PADDED, hidden),
            full(one_rows, hidden),
            full(one_rows, hidden),
            full(count, FIELDS, wide3),
            half(STRIPS, 128),
            half(STRIPS, 128),
            half(STRIPS, 128),
            half(FIELDS, CELLS),
            half(STRIPS, hidden),
            half(STRIPS, hidden),
            half(STRIPS, hidden),
            half(STRIPS, hidden),
            half(STRIPS, hidden),
            half(STRIPS, hidden),
            half(STRIPS, hidden),
            half(STRIPS, hidden),
            half(STRIPS, 128),
            half(STRIPS, 128),
            half(STRIPS, 128),
            full(COUPLED, CELLS),
            full(COUPLED, CELLS),
            full(count // 2, piece_rows, hidden // 2),
            half(count, piece_rows, hidden // 2),
            half(count, piece_rows, hidden // 2),
            full(count, FIELDS, wide3 + hidden // 2),
            half(count, FIELDS, wide3 + hidden // 2),
            half(count, FIELDS, wide3 + hidden // 2),
            full(count, TS, hidden // 2),
            pltpu.SemaphoreType.DMA((copies,)),
            pltpu.SemaphoreType.DMA((copies,)),
            pltpu.SemaphoreType.DMA((2,)),
        ],
        compiler_params=pltpu.CompilerParams(
            collective_id=0, has_side_effects=True, vmem_limit_bytes=48 * 1024 * 1024
        ),
        cost_estimate=pl.CostEstimate(flops=2_000_000_000, bytes_accessed=4_000_000, transcendentals=200_000),
    )(
        turn_table.T,
        state[0],
        cotangent[0],
        land_sea.reshape(1, CELLS),
        w1[0],
        w2[0],
        w3[0].T,
        gates1[0].T,
        gates2[0].T,
        gates3[0].T,
    )
    return (up[None], adj[None], d1[None], d2[:rows].reshape(1, -1), d3.T.reshape(1, -1))


def solution(mesh):
    kernel_spec = P("comp", None, None)
    grid_spec = P("comp", None, "face")
    return jax.shard_map(
        functools.partial(body, mesh.shape["face"]),
        mesh=mesh,
        in_specs=(grid_spec, grid_spec, P("face"), P()) + (kernel_spec,) * 6,
        out_specs=(grid_spec, grid_spec, kernel_spec, P("comp", "face"), P("comp", "face")),
        check_vma=False,
    )
```

```python
import functools

import jax
import jax.numpy as jnp
from jax import lax
from jax.experimental import pallas as pl
from jax.experimental.pallas import tpu as pltpu
from jax.sharding import PartitionSpec as P

FIELDS = 16
COUPLED = 8
ROW_TILES = 4
TS = 16
CELLS = TS * TS
STRIPS = 4 * TS
PADDED = 32
BF = jnp.bfloat16
F32 = jnp.float32

EDGE_MAP = (
    ((0, False), (2, True), (1, True), (3, False)),
    ((1, False), (3, True), (0, True), (2, False)),
    ((2, False), (1, False), (3, True), (0, True)),
    ((3, False), (0, False), (2, True), (1, True)),
)


def nn(x, y):
    return jnp.dot(x, y, preferred_element_type=F32)


def nt(x, y):
    return lax.dot_general(x, y, (((1,), (1,)), ((), ())), preferred_element_type=F32)


def tn(x, y):
    return lax.dot_general(x, y, (((0,), (0,)), ((), ())), preferred_element_type=F32)


def iota(shape, axis):
    return lax.broadcasted_iota(jnp.int32, shape, axis)


def split_low_high(gate, place):
    low = jnp.where(gate >= 5.0, 2.0, jnp.where(gate >= 3.0, 1.0, 0.0))
    high = jnp.where(gate == 0.0, 1.0, jnp.where((gate == 1.0) | (gate == 3.0), 2.0, 3.0))
    return jnp.where(low == place, 1.0, 0.0), jnp.where(high == place, 1.0, 0.0)


def silu_slope(v):
    sig = 1.0 / (1.0 + jnp.exp(-v))
    return v * sig, sig * (1.0 + v * (1.0 - sig))


def slot_pieces(count, groups):
    pieces = []
    for slot in range(count):
        piece, below = 0, count
        for low, size in groups:
            below //= size
            piece += (slot // below % size) << low
        pieces.append(piece)
    return pieces


def stage_groups(count, first):
    bits = count.bit_length() - 1
    groups, low = [], 0
    for width in first + [2] * bits:
        width = min(width, bits - low)
        if width > 0:
            groups.append((low, 1 << width))
            low += width
    return groups


def stage_offsets(count, groups):
    held, start, places = count, 0, []
    for _, size in groups:
        held //= size
        places.append((held, start))
        start += held * (size - 1)
    return places


def kernel(
    count,
    turn_hbm,
    state_hbm,
    cot_hbm,
    sea_hbm,
    w1_hbm,
    w2_hbm,
    w3_hbm,
    gates1_hbm,
    gates2_hbm,
    gates3_hbm,
    up_out,
    adj_out,
    d1_out,
    d2_out,
    d3_out,
    turn,
    state,
    cot,
    sea,
    w1,
    w2,
    w3,
    gates1,
    gates2,
    gates3,
    w2t,
    low2,
    high2,
    cols1,
    cols2,
    shift,
    acts,
    dh,
    w1m,
    w1pad,
    w1p,
    low1,
    high1,
    mask3,
    e0_send,
    e0_own,
    e0_partner,
    e0_inner,
    e1_send,
    e1_recv,
    h2_send,
    h2_recv,
    b2_send,
    b2_recv,
    b1_send,
    b1_recv,
    b0_send,
    b0_own,
    b0_partner,
    b0_inner_send,
    b0_inner,
    big,
    big_send,
    big_recv,
    small,
    small_send,
    small_recv,
    gathered,
    turned,
    send_sem,
    recv_sem,
    load_sem,
):
    big_groups, small_groups = stage_groups(count, [1, 1]), stage_groups(count, [2])
    pieces, small_pieces = slot_pieces(count, big_groups), slot_pieces(count, small_groups)
    taps = w2.shape[0]
    rows = taps // count
    piece_rows = big.shape[1]
    comp = lax.axis_index("comp")
    me = lax.axis_index("face")
    other = 1 - comp
    used = [0]

    def copy_to(src, dst, component, face):
        index = used[0]
        used[0] += 1
        copy = pltpu.make_async_remote_copy(
            src_ref=src,
            dst_ref=dst,
            send_sem=send_sem.at[index],
            recv_sem=recv_sem.at[index],
            device_id=(component, face),
            device_id_type=pl.DeviceIdType.MESH,
        )
        copy.start()
        return copy

    def face_at(offset):
        return lax.rem(me + offset + count, count)

    forward = [face_at(1), face_at(-1), face_at(ROW_TILES), face_at(-ROW_TILES)]
    backward = [forward[1], forward[0], forward[3], forward[2]]

    def digit_of(group):
        low, size = group
        return lax.rem(me // (1 << low), size)

    def mate_of(group, distance):
        low, size = group
        digit = digit_of(group)
        target = lax.rem(digit + distance, size)
        return target, me + (target - digit) * (1 << low)


    barrier = pltpu.get_barrier_semaphore()
    signals = 0
    targets = [(other, me)]
    targets += [(c, f) for c in (comp, other) for f in forward]
    for group in big_groups + small_groups:
        targets += [(comp, mate_of(group, distance)[1]) for distance in range(1, group[1])]
    for target in targets:
        pl.semaphore_signal(barrier, inc=1, device_id=target, device_id_type=pl.DeviceIdType.MESH)
        signals += 1

    loads = []
    for index, (outside, inside) in enumerate(
        (
            (turn_hbm, turn),
            (state_hbm, state),
            (gates3_hbm, gates3),
            (w3_hbm, w3),
            (cot_hbm, cot),
            (sea_hbm, sea),
            (gates1_hbm, gates1),
            (w1_hbm, w1),
            (gates2_hbm, gates2),
            (w2_hbm, w2),
        )
    ):
        load = pltpu.make_async_copy(outside, inside, load_sem.at[index])
        load.start()
        loads.append(load)

    cell = iota((1, CELLS), 1)
    row, column = cell // TS, lax.rem(cell, TS)
    source = iota((CELLS + STRIPS, CELLS), 0)
    for a in range(3):
        for b in range(3):
            r, q = row + (a - 1), column + (b - 1)
            r_in, q_in = (r >= 0) & (r < TS), (q >= 0) & (q < TS)
            at = jnp.where(r_in & q_in, r * TS + q, -1)
            at = jnp.where(r_in & (q < 0), CELLS + r, at)
            at = jnp.where(r_in & (q >= TS), CELLS + TS + r, at)
            at = jnp.where(q_in & (r < 0), CELLS + 2 * TS + q, at)
            at = jnp.where(q_in & (r >= TS), CELLS + 3 * TS + q, at)
            shift[3 * a + b] = jnp.where(source == at, 1.0, 0.0).astype(BF)

    for load in loads[:2]:
        load.wait()
    strip = iota((STRIPS, 1), 0)
    side = strip // TS
    along = lax.rem(strip, TS)
    offsets = (1, -1, ROW_TILES, -ROW_TILES)
    edge_cell = jnp.zeros((STRIPS, 1), jnp.int32)
    for s in range(4):
        turns = turn[s, face_at(offsets[s])]
        for k in range(4):
            slot, flip = EDGE_MAP[s][k]
            j = TS - 1 - along if flip else along
            cell = (j * TS + TS - 1, j * TS, (TS - 1) * TS + j, j)[slot]
            edge_cell = jnp.where((side == s) & (turns == k), cell, edge_cell)
    pick = jnp.where(iota((STRIPS, CELLS), 1) == edge_cell, 1.0, 0.0).astype(BF)

    state_f = state[...].astype(F32)
    wide = jnp.concatenate([state_f, jnp.zeros((128 - FIELDS, CELLS), F32)], 0).astype(BF)
    e0_send[...] = nt(pick, wide).astype(BF)

    pl.semaphore_wait(barrier, signals)
    waits0 = [copy_to(state, e0_inner, other, me)]
    for component, landing in ((comp, e0_own), (other, e0_partner)):
        for s in range(4):
            part = pl.ds(s * TS, TS)
            waits0.append(copy_to(e0_send.at[part], landing.at[part], component, forward[s]))

    for load in loads[2:6]:
        load.wait()
    scale = jnp.where(comp == 1, sea[...].astype(F32), 1.0)
    cot_f = cot[...].astype(F32)
    g3 = (scale * cot_f).astype(BF)
    channel = iota((FIELDS, gates3.shape[1]), 0)
    gate3 = gates3[...].astype(F32)
    group = channel // 4
    gate_rows = jnp.where(
        group == 0,
        gate3[0:1],
        jnp.where(group == 1, gate3[1:2], jnp.where(group == 2, gate3[2:3], gate3[3:4])),
    )
    low3, high3 = split_low_high(gate_rows, lax.rem(channel, 4).astype(F32))
    keep3 = low3 + high3
    w3m = jnp.where(keep3 > 0.0, w3[...].astype(F32), 0.0).astype(BF)
    hidden = w1.shape[1]

    def tap(k):
        return slice(k * hidden, (k + 1) * hidden)

    strips_two = jnp.zeros((STRIPS, hidden), F32)
    for k in range(9):
        edge_grad = nt(shift[k, CELLS:, :], g3).astype(BF)
        strips_two += nn(edge_grad, w3m[:, tap(k)])
    b2_send[...] = strips_two.astype(BF)
    waits_b2 = []
    for s in range(4):
        part = pl.ds(s * TS, TS)
        waits_b2.append(copy_to(b2_send.at[part], b2_recv.at[part], comp, backward[s]))

    for load in loads[6:8]:
        load.wait()
    place = lax.rem(iota((1, hidden), 1), 4).astype(F32)
    spread = jnp.where(iota((hidden // 4, hidden), 0) == iota((hidden // 4, hidden), 1) // 4, 1.0, 0.0)
    spread = spread.astype(BF)
    rows_one = w1.shape[0]
    channels = rows_one // 9
    gate_one = tn(gates1[...].astype(F32).astype(BF), spread)
    lo, hi = split_low_high(gate_one, place)
    low1[...] = jnp.zeros_like(low1)
    high1[...] = jnp.zeros_like(high1)
    low1[pl.ds(0, rows_one)] = lo
    high1[pl.ds(0, rows_one)] = hi
    w1m[...] = jnp.where(lo + hi > 0.0, w1[...].astype(F32), 0.0)
    w1pad[...] = jnp.zeros_like(w1pad)
    for k in range(9):
        w1pad[pl.ds(k * PADDED, channels)] = w1m[pl.ds(k * channels, channels)]
    w1p[...] = w1pad[...].astype(BF)
    w1t = w1pad[...].T.astype(BF)

    for load in loads[8:]:
        load.wait()
    if not rows % TS == 0:
        for ref in (low2, high2, cols1):
            ref[pl.ds(taps, 2 * TS)] = jnp.zeros((2 * TS, hidden), BF)
    def mask_middle(k):
        part = pl.ds(k * hidden, hidden)
        gate = tn(gates2[:, tap(k)].astype(F32).astype(BF), spread)
        lo, hi = split_low_high(gate, place)
        low2[part] = lo.astype(BF)
        high2[part] = hi.astype(BF)
        masked = jnp.where(lo + hi > 0.0, w2[part].astype(F32), 0.0)
        w2[part] = masked.astype(BF)
        w2t[:, tap(k)] = masked.T.astype(BF)

    for k in range(4):
        mask_middle(k)

    def flipped(k):
        return shift[8 - k, :CELLS, :]

    for copy in waits0:
        copy.wait()
    inner = jnp.concatenate(
        [state_f, e0_inner[...].astype(F32)[:COUPLED], jnp.zeros((PADDED - FIELDS - COUPLED, CELLS), F32)], 0
    )
    own_t = e0_own[...].astype(F32).T
    partner_t = e0_partner[...].astype(F32).T
    halo = jnp.concatenate(
        [own_t[:FIELDS], partner_t[:COUPLED], jnp.zeros((PADDED - FIELDS - COUPLED, STRIPS), F32)], 0
    )
    field = jnp.concatenate([inner, halo], 1).astype(BF)
    cols0 = jnp.concatenate([nn(field, shift[k]) for k in range(9)], 0).astype(BF)
    act_one = nn(w1t, cols0)
    hid, slope_one = silu_slope(act_one)
    acts[...] = slope_one
    hid = hid.astype(BF)
    e1_send[...] = nt(pick, hid).astype(BF)
    waits1 = []
    for s in range(4):
        part = pl.ds(s * TS, TS)
        waits1.append(copy_to(e1_send.at[part], e1_recv.at[part], comp, forward[s]))

    for k in range(4, 9):
        mask_middle(k)
    for k in range(9):
        cols1[pl.ds(k * hidden, hidden)] = nn(hid, shift[k, :CELLS, :]).astype(BF)
    shifted3 = jnp.concatenate([nn(g3, flipped(k)) for k in range(9)], 0).astype(BF)
    stacked3 = jnp.concatenate([w3m[:, tap(k)] for k in range(9)], 0)
    dh[...] = tn(stacked3, shifted3)
    for copy in waits_b2:
        copy.wait()
    dh[...] += tn(b2_recv[...], pick)

    for copy in waits1:
        copy.wait()
    halo_t = e1_recv[...].astype(F32).T.astype(BF)
    for k in range(9):
        part = pl.ds(k * hidden, hidden)
        cols1[part] = cols1[part] + nn(halo_t, shift[k, CELLS:, :]).astype(BF)
    act_two = nn(w2t[...], cols1[pl.ds(0, taps)])
    hid, slope_two = silu_slope(act_two)
    g2 = (dh[...] * slope_two).astype(BF)
    hid = hid.astype(BF)

    strips_one = jnp.zeros((STRIPS, hidden), F32)
    for k in range(9):
        edge_grad = nt(shift[k, CELLS:, :], g2).astype(BF)
        strips_one += nt(edge_grad, w2[pl.ds(k * hidden, hidden)])
    b1_send[...] = strips_one.astype(BF)
    h2_send[...] = nt(pick, hid).astype(BF)
    waits_b1, waits_h2 = [], []
    for s in range(4):
        part = pl.ds(s * TS, TS)
        waits_b1.append(copy_to(b1_send.at[part], b1_recv.at[part], comp, backward[s]))
    for s in range(4):
        part = pl.ds(s * TS, TS)
        waits_h2.append(copy_to(h2_send.at[part], h2_recv.at[part], comp, forward[s]))

    lane, packed = iota((hidden, hidden // 2), 0) // 4, iota((hidden, hidden // 2), 1)
    pack_low = jnp.where(lane == packed, 1.0, 0.0).astype(BF)
    pack_high = jnp.where(lane + hidden // 4 == packed, 1.0, 0.0).astype(BF)

    def pack(term, low, high):
        return nn(term * low, pack_low) + nn(term * high, pack_high)

    def unpack(total, low, high):
        top = total.astype(BF)
        rest = (total - top.astype(F32)).astype(BF)
        return (nt(top, pack_low) + nt(rest, pack_low)) * low + (nt(top, pack_high) + nt(rest, pack_high)) * high

    aligned = rows % TS == 0
    slab = rows if aligned else piece_rows + TS

    def piece_part(index):
        return pl.ds(pl.multiple_of(index * rows // TS * TS, TS), slab)

    def settle(values, index):
        if aligned:
            return values
        return pltpu.roll(values, lax.rem(slab - lax.rem(index * rows, TS), slab), 0)[:piece_rows]

    def gather_rows(ref, indices):
        return jnp.concatenate([ref[piece_part(index)] for index in indices], 0)

    def piece_terms(indices):
        term = nt(gather_rows(cols1, indices), g2).astype(BF)
        packed = pack(term, gather_rows(low2, indices), gather_rows(high2, indices))
        return [settle(packed[i * slab : (i + 1) * slab], index) for i, index in enumerate(indices)]

    def start_stage(groups, stage, held, outgoing, landing):
        size, start = stage_offsets(count, groups)[stage]
        group = groups[stage]
        copies = []
        for distance in range(1, group[1]):
            target, mate = mate_of(group, distance)
            at = start + (distance - 1) * size
            for i in range(size):
                outgoing[at + i] = held[target * size + i].astype(BF)
            part = pl.ds(at, size)
            copies.append(copy_to(outgoing.at[part], landing.at[part], comp, mate))
        return copies

    def end_stage(groups, stage, held, landing, copies):
        size, start = stage_offsets(count, groups)[stage]
        mine = digit_of(groups[stage])
        for copy in copies:
            copy.wait()
        for i in range(size):
            total = held[mine * size + i]
            for distance in range(1, groups[stage][1]):
                total = total + landing[start + (distance - 1) * size + i].astype(F32)
            held[i] = total

    half = count // 2
    core = digit_of(big_groups[0])
    for i, packed in enumerate(piece_terms([pieces[i] + (1 - core) for i in range(half)])):
        big_send[i] = packed.astype(BF)
    first = pl.ds(0, half)
    sibling = mate_of(big_groups[0], 1)[1]
    big_copy = copy_to(big_send.at[first], big_recv.at[first], comp, sibling)
    own_terms = piece_terms([pieces[i] + core for i in range(half)])
    big_copy.wait()
    for i, packed in enumerate(own_terms):
        big[i] = packed + big_recv[i].astype(F32)
    big_copies = []
    if len(big_groups) > 1:
        big_copies = start_stage(big_groups, 1, big, big_send, big_recv)

    total = jnp.zeros((hidden, CELLS), F32)
    for k in range(9):
        moved = nn(g2, flipped(k)).astype(BF)
        total += nn(w2[pl.ds(k * hidden, hidden)], moved)
    for k in range(9):
        cols2[pl.ds(k * hidden, hidden)] = nn(hid, shift[k, :CELLS, :]).astype(BF)
    for copy in waits_b1:
        copy.wait()
    total += tn(b1_recv[...], pick)
    g1 = (total * acts[...]).astype(BF)

    back = nn(w1p[...], g1)
    back_zero = jnp.zeros((2 * PADDED, CELLS + STRIPS), F32)
    for k in range(9):
        piece = back[k * PADDED : (k + 1) * PADDED]
        top = piece.astype(BF)
        rest = (piece - top.astype(F32)).astype(BF)
        back_zero += nt(jnp.concatenate([top, rest], 0), shift[k])
    back_zero = back_zero[:PADDED] + back_zero[PADDED:]
    strips_zero = jnp.concatenate([back_zero[:, CELLS:], jnp.zeros((128 - PADDED, STRIPS), F32)], 0).T
    b0_send[...] = strips_zero.astype(BF)
    b0_inner_send[...] = back_zero[FIELDS : FIELDS + COUPLED, :CELLS]
    waits_b0 = [copy_to(b0_inner_send, b0_inner, other, me)]
    for component, landing in ((comp, b0_own), (other, b0_partner)):
        for s in range(4):
            part = pl.ds(s * TS, TS)
            waits_b0.append(copy_to(b0_send.at[part], landing.at[part], component, backward[s]))

    for copy in waits_h2:
        copy.wait()
    halo_t = h2_recv[...].astype(F32).T.astype(BF)
    for k in range(9):
        part = pl.ds(k * hidden, hidden)
        cols2[part] = cols2[part] + nn(halo_t, shift[k, CELLS:, :]).astype(BF)

    term_one = nt(cols0, g1)
    w1pad[...] = term_one
    w1m_rows = [w1pad[pl.ds(k * PADDED, channels)] for k in range(9)]
    w1m_rows.append(jnp.zeros((small.shape[0] * TS - rows_one, hidden), F32))
    term_one = jnp.concatenate(w1m_rows, 0).astype(BF)
    packed_one = pack(term_one, low1[...].astype(BF), high1[...].astype(BF))
    wide3 = small.shape[2] - hidden // 2
    for slot in range(count):
        index = small_pieces[slot]
        part3 = nt(g3, cols2[pl.ds(index * rows, rows)])
        mask3[index, :, pl.ds(0, rows)] = keep3[:, index * rows : (index + 1) * rows]
        small[slot, :, pl.ds(0, rows)] = part3
        small[slot, :, pl.ds(rows, wide3 - rows)] = jnp.zeros((FIELDS, wide3 - rows), F32)
        small[slot, :, pl.ds(wide3, hidden // 2)] = packed_one[index * TS : (index + 1) * TS]
    small_copies = start_stage(small_groups, 0, small, small_send, small_recv)
    result = nn(w3m, cols2[...])
    up_out[...] = (state_f + scale * result).astype(BF)

    for stage in range(max(len(big_groups) - 1, len(small_groups))):
        if stage + 1 < len(big_groups):
            end_stage(big_groups, stage + 1, big, big_recv, big_copies)
            if stage + 2 < len(big_groups):
                big_copies = start_stage(big_groups, stage + 2, big, big_send, big_recv)
        if stage < len(small_groups):
            end_stage(small_groups, stage, small, small_recv, small_copies)
            if stage + 1 < len(small_groups):
                small_copies = start_stage(small_groups, stage + 1, small, small_send, small_recv)

    places = stage_offsets(count, small_groups)
    my_slot = jnp.int32(0)
    for group, (size, _) in zip(small_groups, places):
        my_slot = my_slot + digit_of(group) * size
    gathered[my_slot] = small[0, :, pl.ds(wide3, hidden // 2)]
    start = my_slot
    for stage in range(len(small_groups) - 1, -1, -1):
        group, size = small_groups[stage], places[stage][0]
        part = pl.ds(start, size)
        copies = [
            copy_to(gathered.at[part], gathered.at[part], comp, mate_of(group, distance)[1])
            for distance in range(1, group[1])
        ]
        if stage == len(small_groups) - 1:
            mine3 = small[0, :, pl.ds(0, rows)] * mask3[me, :, pl.ds(0, rows)]
            if rows % 8 == 0:
                turned[...] = jnp.concatenate([mine3, jnp.zeros((128 - FIELDS, rows), F32)], 0).T
                lines = jnp.concatenate(
                    [turned[pl.ds(u, rows // 8, stride=8), :][:, :FIELDS] for u in range(8)], 1
                )
                for j in range(rows // 8):
                    d3_out[:, pl.ds(j * 128, 128)] = lines[j : j + 1]
            else:
                d3_out[...] = mine3
            part = piece_part(me)
            low_mine, high_mine = (settle(ref[part].astype(F32), me) for ref in (low2, high2))
            mine2 = unpack(big[0], low_mine, high_mine)
            for side in range(2):
                d2_out[pl.ds(side, piece_rows, stride=2), :] = mine2[:, side * 128 : (side + 1) * 128]
            for waiting in waits_b0:
                waiting.wait()
            returned = tn(b0_own[...], pick)
            coupled = tn(b0_partner[...], pick)
            own = cot_f + back_zero[:FIELDS, :CELLS] + returned[:FIELDS]
            top = own[:COUPLED] + b0_inner[...] + coupled[FIELDS : FIELDS + COUPLED]
            adj_out[...] = jnp.concatenate([top, own[COUPLED:]], 0)
        for copy in copies:
            copy.wait()
        start = start - digit_of(group) * size
    slot_of = [small_pieces.index(index) for index in range(count)]
    summed = jnp.concatenate([gathered[slot_of[i]] for i in range(-(-rows_one // TS))], 0)
    kept = summed.shape[0]
    whole = unpack(summed, low1[pl.ds(0, kept)], high1[pl.ds(0, kept)])
    d1_out[...] = whole[:rows_one]


def body(count, state, cotangent, land_sea, turn_table, w1, w2, w3, gates1, gates2, gates3):
    hidden = w1.shape[2]
    taps = w2.shape[1]
    rows = taps // count
    piece_rows = -(-rows // TS) * TS
    spare = taps if rows % TS == 0 else taps + 2 * TS
    wide3 = -(-rows // 128) * 128
    one_rows = max(count * TS, 256)
    vmem = pl.BlockSpec(memory_space=pltpu.VMEM)
    any_space = pl.BlockSpec(memory_space=pl.ANY)
    copies = 34
    for groups, times in ((stage_groups(count, [1, 1]), 1), (stage_groups(count, [2]), 2)):
        copies += times * sum(size - 1 for _, size in groups)
    hbm = pl.BlockSpec(memory_space=pltpu.HBM)
    shape3 = (1, rows * FIELDS) if rows % 8 == 0 else (FIELDS, rows)

    def half(*shape):
        return pltpu.VMEM(shape, BF)

    def full(*shape):
        return pltpu.VMEM(shape, F32)

    up, adj, d1, d2, d3 = pl.pallas_call(
        functools.partial(kernel, count),
        out_shape=(
            jax.ShapeDtypeStruct((FIELDS, CELLS), BF),
            jax.ShapeDtypeStruct((FIELDS, CELLS), F32),
            jax.ShapeDtypeStruct((w1.shape[1], hidden), F32),
            jax.ShapeDtypeStruct((2 * piece_rows, 128), F32),
            jax.ShapeDtypeStruct(shape3, F32),
        ),
        in_specs=[hbm] * 10,
        out_specs=(vmem,) * 5,
        scratch_shapes=[
            pltpu.SMEM(turn_table.shape[::-1], jnp.int32),
            half(FIELDS, CELLS),
            half(FIELDS, CELLS),
            pltpu.VMEM((1, CELLS), jnp.int32),
            half(w1.shape[1], hidden),
            half(taps, hidden),
            half(FIELDS, taps),
            pltpu.VMEM((hidden // 4, w1.shape[1]), jnp.int32),
            pltpu.VMEM((hidden // 4, taps), jnp.int32),
            pltpu.VMEM((FIELDS // 4, taps), jnp.int32),
            half(hidden, taps),
            half(spare, hidden),
            half(spare, hidden),
            half(spare, hidden),
            half(taps, hidden),
            half(9, CELLS + STRIPS, CELLS),
            full(hidden, CELLS),
            full(hidden, CELLS),
            full(w1.shape[1], hidden),
            full(9 * PADDED, hidden),
            half(9 * PADDED, hidden),
            full(one_rows, hidden),
            full(one_rows, hidden),
            full(count, FIELDS, wide3),
            half(STRIPS, 128),
            half(STRIPS, 128),
            half(STRIPS, 128),
            half(FIELDS, CELLS),
            half(STRIPS, hidden),
            half(STRIPS, hidden),
            half(STRIPS, hidden),
            half(STRIPS, hidden),
            half(STRIPS, hidden),
            half(STRIPS, hidden),
            half(STRIPS, hidden),
            half(STRIPS, hidden),
            half(STRIPS, 128),
            half(STRIPS, 128),
            half(STRIPS, 128),
            full(COUPLED, CELLS),
            full(COUPLED, CELLS),
            full(count // 2, piece_rows, hidden // 2),
            half(count, piece_rows, hidden // 2),
            half(count, piece_rows, hidden // 2),
            full(count, FIELDS, wide3 + hidden // 2),
            half(count, FIELDS, wide3 + hidden // 2),
            half(count, FIELDS, wide3 + hidden // 2),
            full(count, TS, hidden // 2),
            full(rows, 128),
            pltpu.SemaphoreType.DMA((copies,)),
            pltpu.SemaphoreType.DMA((copies,)),
            pltpu.SemaphoreType.DMA((10,)),
        ],
        compiler_params=pltpu.CompilerParams(
            collective_id=0, has_side_effects=True, vmem_limit_bytes=64 * 1024 * 1024
        ),
        cost_estimate=pl.CostEstimate(flops=2_000_000_000, bytes_accessed=4_000_000, transcendentals=200_000),
    )(
        turn_table.T,
        state[0],
        cotangent[0],
        land_sea.reshape(1, CELLS),
        w1[0],
        w2[0],
        w3[0].T,
        gates1[0].T,
        gates2[0].T,
        gates3[0].T,
    )
    results = (up, adj, d1, d2, d3)
    lead = (1, 1, 1, 0, 0)

    def write_all(*refs):
        copies = []
        for index in range(5):
            target = refs[5 + index].at[0] if lead[index] else refs[5 + index]
            copies.append(pltpu.make_async_copy(refs[index], target, refs[10].at[index]))
            copies[-1].start()
        for copy in copies:
            copy.wait()

    up, adj, d1, d2, d3 = pl.pallas_call(
        write_all,
        out_shape=tuple(
            jax.ShapeDtypeStruct((1,) * extra + value.shape, value.dtype) for extra, value in zip(lead, results)
        ),
        in_specs=[any_space] * 5,
        out_specs=(hbm,) * 5,
        scratch_shapes=[pltpu.SemaphoreType.DMA((5,))],
        compiler_params=pltpu.CompilerParams(vmem_limit_bytes=64 * 1024 * 1024),
    )(*results)
    if rows % 8:
        d3 = d3.T
    return (up, adj, d1, d2.reshape(1, -1)[:, : rows * hidden], d3.reshape(1, -1))


def solution(mesh):
    kernel_spec = P("comp", None, None)
    grid_spec = P("comp", None, "face")
    return jax.shard_map(
        functools.partial(body, mesh.shape["face"]),
        mesh=mesh,
        in_specs=(grid_spec, grid_spec, P("face"), P()) + (kernel_spec,) * 6,
        out_specs=(grid_spec, grid_spec, kernel_spec, P("comp", "face"), P("comp", "face")),
        check_vma=False,
    )
```

```python
import functools

import jax
import jax.numpy as jnp
from jax import lax
from jax.experimental import pallas as pl
from jax.experimental.pallas import tpu as pltpu
from jax.sharding import PartitionSpec as P

FIELDS = 16
COUPLED = 8
ROW_TILES = 4
TS = 16
CELLS = TS * TS
STRIPS = 4 * TS
PADDED = 32
BF = jnp.bfloat16
F32 = jnp.float32

EDGE_MAP = (
    ((0, False), (2, True), (1, True), (3, False)),
    ((1, False), (3, True), (0, True), (2, False)),
    ((2, False), (1, False), (3, True), (0, True)),
    ((3, False), (0, False), (2, True), (1, True)),
)


def nn(x, y):
    return jnp.dot(x, y, preferred_element_type=F32)


def nt(x, y):
    return lax.dot_general(x, y, (((1,), (1,)), ((), ())), preferred_element_type=F32)


def tn(x, y):
    return lax.dot_general(x, y, (((0,), (0,)), ((), ())), preferred_element_type=F32)


def iota(shape, axis):
    return lax.broadcasted_iota(jnp.int32, shape, axis)


def split_low_high(gate, place):
    low = jnp.where(gate >= 5.0, 2.0, jnp.where(gate >= 3.0, 1.0, 0.0))
    high = jnp.where(gate == 0.0, 1.0, jnp.where((gate == 1.0) | (gate == 3.0), 2.0, 3.0))
    return jnp.where(low == place, 1.0, 0.0), jnp.where(high == place, 1.0, 0.0)


def silu_slope(v):
    sig = 1.0 / (1.0 + jnp.exp(-v))
    return v * sig, sig * (1.0 + v * (1.0 - sig))


def slot_pieces(count, groups):
    pieces = []
    for slot in range(count):
        piece, below = 0, count
        for low, size in groups:
            below //= size
            piece += (slot // below % size) << low
        pieces.append(piece)
    return pieces


def stage_groups(count, first):
    bits = count.bit_length() - 1
    groups, low = [], 0
    for width in first + [2] * bits:
        width = min(width, bits - low)
        if width > 0:
            groups.append((low, 1 << width))
            low += width
    return groups


def stage_offsets(count, groups):
    held, start, places = count, 0, []
    for _, size in groups:
        held //= size
        places.append((held, start))
        start += held * (size - 1)
    return places


def kernel(
    count,
    turn_hbm,
    state_hbm,
    cot_hbm,
    sea_hbm,
    w1_hbm,
    w2_hbm,
    w3_hbm,
    gates1_hbm,
    gates2_hbm,
    gates3_hbm,
    up_out,
    adj_out,
    d1_out,
    d2_out,
    d3_out,
    turn,
    state,
    cot,
    sea,
    w1,
    w2,
    w3,
    gates1,
    gates2,
    gates3,
    w2t,
    low2,
    high2,
    cols1,
    cols2,
    shift,
    acts,
    dh,
    w1m,
    w1pad,
    w1p,
    low1,
    high1,
    mask3,
    e0_send,
    e0_own,
    e0_partner,
    e0_inner,
    e1_send,
    e1_recv,
    h2_send,
    h2_recv,
    b2_send,
    b2_recv,
    b1_send,
    b1_recv,
    b0_send,
    b0_own,
    b0_partner,
    b0_inner_send,
    b0_inner,
    big,
    big_send,
    big_recv,
    one,
    one_send,
    one_recv,
    three,
    three_send,
    three_recv,
    gathered,
    turned,
    send_sem,
    recv_sem,
    load_sem,
):
    big_groups, small_groups = stage_groups(count, [1, 1]), stage_groups(count, [2])
    pieces, small_pieces = slot_pieces(count, big_groups), slot_pieces(count, small_groups)
    taps = w2.shape[0]
    rows = taps // count
    piece_rows = big.shape[1]
    comp = lax.axis_index("comp")
    me = lax.axis_index("face")
    other = 1 - comp
    used = [0]

    def copy_to(src, dst, component, face):
        index = used[0]
        used[0] += 1
        copy = pltpu.make_async_remote_copy(
            src_ref=src,
            dst_ref=dst,
            send_sem=send_sem.at[index],
            recv_sem=recv_sem.at[index],
            device_id=(component, face),
            device_id_type=pl.DeviceIdType.MESH,
        )
        copy.start()
        return copy

    def face_at(offset):
        return lax.rem(me + offset + count, count)

    forward = [face_at(1), face_at(-1), face_at(ROW_TILES), face_at(-ROW_TILES)]
    backward = [forward[1], forward[0], forward[3], forward[2]]

    def digit_of(group):
        low, size = group
        return lax.rem(me // (1 << low), size)

    def mate_of(group, distance):
        low, size = group
        digit = digit_of(group)
        target = lax.rem(digit + distance, size)
        return target, me + (target - digit) * (1 << low)


    barrier = pltpu.get_barrier_semaphore()
    signals = 0
    targets = [(other, me)]
    targets += [(c, f) for c in (comp, other) for f in forward]
    for group in big_groups + small_groups:
        targets += [(comp, mate_of(group, distance)[1]) for distance in range(1, group[1])]
    for target in targets:
        pl.semaphore_signal(barrier, inc=1, device_id=target, device_id_type=pl.DeviceIdType.MESH)
        signals += 1

    loads = []
    for index, (outside, inside) in enumerate(
        (
            (turn_hbm, turn),
            (state_hbm, state),
            (gates3_hbm, gates3),
            (w3_hbm, w3),
            (cot_hbm, cot),
            (sea_hbm, sea),
            (gates1_hbm, gates1),
            (w1_hbm, w1),
            (gates2_hbm, gates2),
            (w2_hbm, w2),
        )
    ):
        load = pltpu.make_async_copy(outside, inside, load_sem.at[index])
        load.start()
        loads.append(load)

    cell = iota((1, CELLS), 1)
    row, column = cell // TS, lax.rem(cell, TS)
    source = iota((CELLS + STRIPS, CELLS), 0)
    for a in range(3):
        for b in range(3):
            r, q = row + (a - 1), column + (b - 1)
            r_in, q_in = (r >= 0) & (r < TS), (q >= 0) & (q < TS)
            at = jnp.where(r_in & q_in, r * TS + q, -1)
            at = jnp.where(r_in & (q < 0), CELLS + r, at)
            at = jnp.where(r_in & (q >= TS), CELLS + TS + r, at)
            at = jnp.where(q_in & (r < 0), CELLS + 2 * TS + q, at)
            at = jnp.where(q_in & (r >= TS), CELLS + 3 * TS + q, at)
            shift[3 * a + b] = jnp.where(source == at, 1.0, 0.0).astype(BF)

    for load in loads[:2]:
        load.wait()
    strip = iota((STRIPS, 1), 0)
    side = strip // TS
    along = lax.rem(strip, TS)
    offsets = (1, -1, ROW_TILES, -ROW_TILES)
    edge_cell = jnp.zeros((STRIPS, 1), jnp.int32)
    for s in range(4):
        turns = turn[s, face_at(offsets[s])]
        for k in range(4):
            slot, flip = EDGE_MAP[s][k]
            j = TS - 1 - along if flip else along
            cell = (j * TS + TS - 1, j * TS, (TS - 1) * TS + j, j)[slot]
            edge_cell = jnp.where((side == s) & (turns == k), cell, edge_cell)
    pick = jnp.where(iota((STRIPS, CELLS), 1) == edge_cell, 1.0, 0.0).astype(BF)

    state_f = state[...].astype(F32)
    wide = jnp.concatenate([state_f, jnp.zeros((128 - FIELDS, CELLS), F32)], 0).astype(BF)
    e0_send[...] = nt(pick, wide).astype(BF)

    pl.semaphore_wait(barrier, signals)
    waits0 = [copy_to(state, e0_inner, other, me)]
    for component, landing in ((comp, e0_own), (other, e0_partner)):
        for s in range(4):
            part = pl.ds(s * TS, TS)
            waits0.append(copy_to(e0_send.at[part], landing.at[part], component, forward[s]))

    for load in loads[2:6]:
        load.wait()
    scale = jnp.where(comp == 1, sea[...].astype(F32), 1.0)
    cot_f = cot[...].astype(F32)
    g3 = (scale * cot_f).astype(BF)
    channel = iota((FIELDS, gates3.shape[1]), 0)
    gate3 = gates3[...].astype(F32)
    group = channel // 4
    gate_rows = jnp.where(
        group == 0,
        gate3[0:1],
        jnp.where(group == 1, gate3[1:2], jnp.where(group == 2, gate3[2:3], gate3[3:4])),
    )
    low3, high3 = split_low_high(gate_rows, lax.rem(channel, 4).astype(F32))
    keep3 = low3 + high3
    w3m = jnp.where(keep3 > 0.0, w3[...].astype(F32), 0.0).astype(BF)
    hidden = w1.shape[1]

    def tap(k):
        return slice(k * hidden, (k + 1) * hidden)

    strips_two = jnp.zeros((STRIPS, hidden), F32)
    for k in range(9):
        edge_grad = nt(shift[k, CELLS:, :], g3).astype(BF)
        strips_two += nn(edge_grad, w3m[:, tap(k)])
    b2_send[...] = strips_two.astype(BF)
    waits_b2 = []
    for s in range(4):
        part = pl.ds(s * TS, TS)
        waits_b2.append(copy_to(b2_send.at[part], b2_recv.at[part], comp, backward[s]))

    for load in loads[6:8]:
        load.wait()
    place = lax.rem(iota((1, hidden), 1), 4).astype(F32)
    spread = jnp.where(iota((hidden // 4, hidden), 0) == iota((hidden // 4, hidden), 1) // 4, 1.0, 0.0)
    spread = spread.astype(BF)
    rows_one = w1.shape[0]
    channels = rows_one // 9
    gate_one = tn(gates1[...].astype(F32).astype(BF), spread)
    lo, hi = split_low_high(gate_one, place)
    low1[...] = jnp.zeros_like(low1)
    high1[...] = jnp.zeros_like(high1)
    low1[pl.ds(0, rows_one)] = lo
    high1[pl.ds(0, rows_one)] = hi
    w1m[...] = jnp.where(lo + hi > 0.0, w1[...].astype(F32), 0.0)
    w1pad[...] = jnp.zeros_like(w1pad)
    for k in range(9):
        w1pad[pl.ds(k * PADDED, channels)] = w1m[pl.ds(k * channels, channels)]
    w1p[...] = w1pad[...].astype(BF)
    w1t = w1pad[...].T.astype(BF)

    for load in loads[8:]:
        load.wait()
    if not rows % TS == 0:
        for ref in (low2, high2, cols1):
            ref[pl.ds(taps, 2 * TS)] = jnp.zeros((2 * TS, hidden), BF)
    def mask_middle(k):
        part = pl.ds(k * hidden, hidden)
        gate = tn(gates2[:, tap(k)].astype(F32).astype(BF), spread)
        lo, hi = split_low_high(gate, place)
        low2[part] = lo.astype(BF)
        high2[part] = hi.astype(BF)
        masked = jnp.where(lo + hi > 0.0, w2[part].astype(F32), 0.0)
        w2[part] = masked.astype(BF)
        w2t[:, tap(k)] = masked.T.astype(BF)

    for k in range(4):
        mask_middle(k)

    def flipped(k):
        return shift[8 - k, :CELLS, :]

    for copy in waits0:
        copy.wait()
    inner = jnp.concatenate(
        [state_f, e0_inner[...].astype(F32)[:COUPLED], jnp.zeros((PADDED - FIELDS - COUPLED, CELLS), F32)], 0
    )
    own_t = e0_own[...].astype(F32).T
    partner_t = e0_partner[...].astype(F32).T
    halo = jnp.concatenate(
        [own_t[:FIELDS], partner_t[:COUPLED], jnp.zeros((PADDED - FIELDS - COUPLED, STRIPS), F32)], 0
    )
    field = jnp.concatenate([inner, halo], 1).astype(BF)
    cols0 = jnp.concatenate([nn(field, shift[k]) for k in range(9)], 0).astype(BF)
    act_one = nn(w1t, cols0)
    hid, slope_one = silu_slope(act_one)
    acts[...] = slope_one
    hid = hid.astype(BF)
    e1_send[...] = nt(pick, hid).astype(BF)
    waits1 = []
    for s in range(4):
        part = pl.ds(s * TS, TS)
        waits1.append(copy_to(e1_send.at[part], e1_recv.at[part], comp, forward[s]))

    for k in range(4, 9):
        mask_middle(k)
    for k in range(9):
        cols1[pl.ds(k * hidden, hidden)] = nn(hid, shift[k, :CELLS, :]).astype(BF)
    shifted3 = jnp.concatenate([nn(g3, flipped(k)) for k in range(9)], 0).astype(BF)
    stacked3 = jnp.concatenate([w3m[:, tap(k)] for k in range(9)], 0)
    dh[...] = tn(stacked3, shifted3)
    for copy in waits_b2:
        copy.wait()
    dh[...] += tn(b2_recv[...], pick)

    for copy in waits1:
        copy.wait()
    halo_t = e1_recv[...].astype(F32).T.astype(BF)
    for k in range(9):
        part = pl.ds(k * hidden, hidden)
        cols1[part] = cols1[part] + nn(halo_t, shift[k, CELLS:, :]).astype(BF)
    act_two = nn(w2t[...], cols1[pl.ds(0, taps)])
    hid, slope_two = silu_slope(act_two)
    g2 = (dh[...] * slope_two).astype(BF)
    hid = hid.astype(BF)

    strips_one = jnp.zeros((STRIPS, hidden), F32)
    for k in range(9):
        edge_grad = nt(shift[k, CELLS:, :], g2).astype(BF)
        strips_one += nt(edge_grad, w2[pl.ds(k * hidden, hidden)])
    b1_send[...] = strips_one.astype(BF)
    h2_send[...] = nt(pick, hid).astype(BF)
    waits_b1, waits_h2 = [], []
    for s in range(4):
        part = pl.ds(s * TS, TS)
        waits_b1.append(copy_to(b1_send.at[part], b1_recv.at[part], comp, backward[s]))
    for s in range(4):
        part = pl.ds(s * TS, TS)
        waits_h2.append(copy_to(h2_send.at[part], h2_recv.at[part], comp, forward[s]))

    lane, packed = iota((hidden, hidden // 2), 0) // 4, iota((hidden, hidden // 2), 1)
    pack_low = jnp.where(lane == packed, 1.0, 0.0).astype(BF)
    pack_high = jnp.where(lane + hidden // 4 == packed, 1.0, 0.0).astype(BF)

    def pack(term, low, high):
        return nn(term * low, pack_low) + nn(term * high, pack_high)

    def unpack(total, low, high):
        top = total.astype(BF)
        rest = (total - top.astype(F32)).astype(BF)
        return (nt(top, pack_low) + nt(rest, pack_low)) * low + (nt(top, pack_high) + nt(rest, pack_high)) * high

    aligned = rows % TS == 0
    slab = rows if aligned else piece_rows + TS

    def piece_part(index):
        return pl.ds(pl.multiple_of(index * rows // TS * TS, TS), slab)

    def settle(values, index):
        if aligned:
            return values
        return pltpu.roll(values, lax.rem(slab - lax.rem(index * rows, TS), slab), 0)[:piece_rows]

    def gather_rows(ref, indices):
        return jnp.concatenate([ref[piece_part(index)] for index in indices], 0)

    def piece_terms(indices):
        term = nt(gather_rows(cols1, indices), g2).astype(BF)
        packed = pack(term, gather_rows(low2, indices), gather_rows(high2, indices))
        return [settle(packed[i * slab : (i + 1) * slab], index) for i, index in enumerate(indices)]

    def start_stage(groups, stage, held, outgoing, landing):
        size, start = stage_offsets(count, groups)[stage]
        group = groups[stage]
        copies = []
        for distance in range(1, group[1]):
            target, mate = mate_of(group, distance)
            at = start + (distance - 1) * size
            for i in range(size):
                outgoing[at + i] = held[target * size + i].astype(BF)
            part = pl.ds(at, size)
            copies.append(copy_to(outgoing.at[part], landing.at[part], comp, mate))
        return copies

    def end_stage(groups, stage, held, landing, copies):
        size, start = stage_offsets(count, groups)[stage]
        mine = digit_of(groups[stage])
        for copy in copies:
            copy.wait()
        for i in range(size):
            total = held[mine * size + i]
            for distance in range(1, groups[stage][1]):
                total = total + landing[start + (distance - 1) * size + i].astype(F32)
            held[i] = total

    half = count // 2
    core = digit_of(big_groups[0])
    for i, packed in enumerate(piece_terms([pieces[i] + (1 - core) for i in range(half)])):
        big_send[i] = packed.astype(BF)
    first = pl.ds(0, half)
    sibling = mate_of(big_groups[0], 1)[1]
    big_copy = copy_to(big_send.at[first], big_recv.at[first], comp, sibling)
    own_terms = piece_terms([pieces[i] + core for i in range(half)])
    big_copy.wait()
    for i, packed in enumerate(own_terms):
        big[i] = packed + big_recv[i].astype(F32)
    big_copies = []
    if len(big_groups) > 1:
        big_copies = start_stage(big_groups, 1, big, big_send, big_recv)

    total = jnp.zeros((hidden, CELLS), F32)
    for k in range(9):
        moved = nn(g2, flipped(k)).astype(BF)
        total += nn(w2[pl.ds(k * hidden, hidden)], moved)
    for copy in waits_b1:
        copy.wait()
    total += tn(b1_recv[...], pick)
    g1 = (total * acts[...]).astype(BF)

    one_rows = low1.shape[0]
    term_one = nt(cols0, g1)
    w1pad[...] = term_one
    w1m_rows = [w1pad[pl.ds(k * PADDED, channels)] for k in range(9)]
    w1m_rows.append(jnp.zeros((one_rows - rows_one, hidden), F32))
    term_one = jnp.concatenate(w1m_rows, 0).astype(BF)
    packed_one = pack(term_one, low1[...].astype(BF), high1[...].astype(BF))
    for slot in range(count):
        index = small_pieces[slot]
        one[slot] = packed_one[index * TS : (index + 1) * TS]
    one_copies = start_stage(small_groups, 0, one, one_send, one_recv)

    back = nn(w1p[...], g1)
    back_zero = jnp.zeros((2 * PADDED, CELLS + STRIPS), F32)
    for k in range(9):
        piece = back[k * PADDED : (k + 1) * PADDED]
        top = piece.astype(BF)
        rest = (piece - top.astype(F32)).astype(BF)
        back_zero += nt(jnp.concatenate([top, rest], 0), shift[k])
    back_zero = back_zero[:PADDED] + back_zero[PADDED:]
    strips_zero = jnp.concatenate([back_zero[:, CELLS:], jnp.zeros((128 - PADDED, STRIPS), F32)], 0).T
    b0_send[...] = strips_zero.astype(BF)
    b0_inner_send[...] = back_zero[FIELDS : FIELDS + COUPLED, :CELLS]
    waits_b0 = [copy_to(b0_inner_send, b0_inner, other, me)]
    for component, landing in ((comp, b0_own), (other, b0_partner)):
        for s in range(4):
            part = pl.ds(s * TS, TS)
            waits_b0.append(copy_to(b0_send.at[part], landing.at[part], component, backward[s]))

    if len(big_groups) > 1:
        end_stage(big_groups, 1, big, big_recv, big_copies)
        if len(big_groups) > 2:
            big_copies = start_stage(big_groups, 2, big, big_send, big_recv)

    for k in range(9):
        cols2[pl.ds(k * hidden, hidden)] = nn(hid, shift[k, :CELLS, :]).astype(BF)
    for copy in waits_h2:
        copy.wait()
    halo_t = h2_recv[...].astype(F32).T.astype(BF)
    for k in range(9):
        part = pl.ds(k * hidden, hidden)
        cols2[part] = cols2[part] + nn(halo_t, shift[k, CELLS:, :]).astype(BF)

    end_stage(small_groups, 0, one, one_recv, one_copies)
    if len(small_groups) > 1:
        one_copies = start_stage(small_groups, 1, one, one_send, one_recv)

    wide3 = three.shape[2]
    for slot in range(count):
        index = small_pieces[slot]
        mask3[index, :, pl.ds(0, rows)] = keep3[:, index * rows : (index + 1) * rows]
        three[slot, :, pl.ds(0, rows)] = nt(g3, cols2[pl.ds(index * rows, rows)])
        if wide3 > rows:
            three[slot, :, pl.ds(rows, wide3 - rows)] = jnp.zeros((FIELDS, wide3 - rows), F32)
    three_copies = start_stage(small_groups, 0, three, three_send, three_recv)

    for stage in range(1, len(small_groups)):
        end_stage(small_groups, stage, one, one_recv, one_copies)
        if stage + 1 < len(small_groups):
            one_copies = start_stage(small_groups, stage + 1, one, one_send, one_recv)

    places = stage_offsets(count, small_groups)
    my_slot = jnp.int32(0)
    for group, (size, _) in zip(small_groups, places):
        my_slot = my_slot + digit_of(group) * size
    gathered[my_slot] = one[0]
    start = my_slot
    for stage in range(len(small_groups) - 1, -1, -1):
        group, size = small_groups[stage], places[stage][0]
        part = pl.ds(start, size)
        copies = [
            copy_to(gathered.at[part], gathered.at[part], comp, mate_of(group, distance)[1])
            for distance in range(1, group[1])
        ]
        if stage == len(small_groups) - 1:
            result = nn(w3m, cols2[...])
            up_out[...] = (state_f + scale * result).astype(BF)
            end_stage(small_groups, 0, three, three_recv, three_copies)
            if len(small_groups) > 1:
                three_copies = start_stage(small_groups, 1, three, three_send, three_recv)
        if stage == 0:
            for step in range(1, len(small_groups)):
                end_stage(small_groups, step, three, three_recv, three_copies)
                if step + 1 < len(small_groups):
                    three_copies = start_stage(small_groups, step + 1, three, three_send, three_recv)
            for step in range(2, len(big_groups)):
                end_stage(big_groups, step, big, big_recv, big_copies)
                if step + 1 < len(big_groups):
                    big_copies = start_stage(big_groups, step + 1, big, big_send, big_recv)
            mine3 = three[0, :, pl.ds(0, rows)] * mask3[me, :, pl.ds(0, rows)]
            if rows % 8 == 0:
                turned[...] = jnp.concatenate([mine3, jnp.zeros((128 - FIELDS, rows), F32)], 0).T
                lines = jnp.concatenate(
                    [turned[pl.ds(u, rows // 8, stride=8), :][:, :FIELDS] for u in range(8)], 1
                )
                for j in range(rows // 8):
                    d3_out[:, pl.ds(j * 128, 128)] = lines[j : j + 1]
            else:
                d3_out[...] = mine3
            part = piece_part(me)
            low_mine, high_mine = (settle(ref[part].astype(F32), me) for ref in (low2, high2))
            mine2 = unpack(big[0], low_mine, high_mine)
            for side in range(2):
                d2_out[pl.ds(side, piece_rows, stride=2), :] = mine2[:, side * 128 : (side + 1) * 128]
            for waiting in waits_b0:
                waiting.wait()
            returned = tn(b0_own[...], pick)
            coupled = tn(b0_partner[...], pick)
            own = cot_f + back_zero[:FIELDS, :CELLS] + returned[:FIELDS]
            top = own[:COUPLED] + b0_inner[...] + coupled[FIELDS : FIELDS + COUPLED]
            adj_out[...] = jnp.concatenate([top, own[COUPLED:]], 0)
        for copy in copies:
            copy.wait()
        start = start - digit_of(group) * size
    slot_of = [small_pieces.index(index) for index in range(count)]
    summed = jnp.concatenate([gathered[slot_of[i]] for i in range(-(-rows_one // TS))], 0)
    kept = summed.shape[0]
    whole = unpack(summed, low1[pl.ds(0, kept)], high1[pl.ds(0, kept)])
    d1_out[...] = whole[:rows_one]


def body(count, state, cotangent, land_sea, turn_table, w1, w2, w3, gates1, gates2, gates3):
    hidden = w1.shape[2]
    taps = w2.shape[1]
    rows = taps // count
    piece_rows = -(-rows // TS) * TS
    spare = taps if rows % TS == 0 else taps + 2 * TS
    wide3 = -(-rows // 128) * 128
    one_rows = max(count * TS, 256)
    vmem = pl.BlockSpec(memory_space=pltpu.VMEM)
    any_space = pl.BlockSpec(memory_space=pl.ANY)
    copies = 34
    for groups, times in ((stage_groups(count, [1, 1]), 1), (stage_groups(count, [2]), 3)):
        copies += times * sum(size - 1 for _, size in groups)
    hbm = pl.BlockSpec(memory_space=pltpu.HBM)
    shape3 = (1, rows * FIELDS) if rows % 8 == 0 else (FIELDS, rows)

    def half(*shape):
        return pltpu.VMEM(shape, BF)

    def full(*shape):
        return pltpu.VMEM(shape, F32)

    up, adj, d1, d2, d3 = pl.pallas_call(
        functools.partial(kernel, count),
        out_shape=(
            jax.ShapeDtypeStruct((FIELDS, CELLS), BF),
            jax.ShapeDtypeStruct((FIELDS, CELLS), F32),
            jax.ShapeDtypeStruct((w1.shape[1], hidden), F32),
            jax.ShapeDtypeStruct((2 * piece_rows, 128), F32),
            jax.ShapeDtypeStruct(shape3, F32),
        ),
        in_specs=[hbm] * 10,
        out_specs=(vmem,) * 5,
        scratch_shapes=[
            pltpu.SMEM(turn_table.shape[::-1], jnp.int32),
            half(FIELDS, CELLS),
            half(FIELDS, CELLS),
            pltpu.VMEM((1, CELLS), jnp.int32),
            half(w1.shape[1], hidden),
            half(taps, hidden),
            half(FIELDS, taps),
            pltpu.VMEM((hidden // 4, w1.shape[1]), jnp.int32),
            pltpu.VMEM((hidden // 4, taps), jnp.int32),
            pltpu.VMEM((FIELDS // 4, taps), jnp.int32),
            half(hidden, taps),
            half(spare, hidden),
            half(spare, hidden),
            half(spare, hidden),
            half(taps, hidden),
            half(9, CELLS + STRIPS, CELLS),
            full(hidden, CELLS),
            full(hidden, CELLS),
            full(w1.shape[1], hidden),
            full(9 * PADDED, hidden),
            half(9 * PADDED, hidden),
            full(one_rows, hidden),
            full(one_rows, hidden),
            full(count, FIELDS, wide3),
            half(STRIPS, 128),
            half(STRIPS, 128),
            half(STRIPS, 128),
            half(FIELDS, CELLS),
            half(STRIPS, hidden),
            half(STRIPS, hidden),
            half(STRIPS, hidden),
            half(STRIPS, hidden),
            half(STRIPS, hidden),
            half(STRIPS, hidden),
            half(STRIPS, hidden),
            half(STRIPS, hidden),
            half(STRIPS, 128),
            half(STRIPS, 128),
            half(STRIPS, 128),
            full(COUPLED, CELLS),
            full(COUPLED, CELLS),
            full(count // 2, piece_rows, hidden // 2),
            half(count, piece_rows, hidden // 2),
            half(count, piece_rows, hidden // 2),
            full(count, TS, hidden // 2),
            half(count, TS, hidden // 2),
            half(count, TS, hidden // 2),
            full(count, FIELDS, wide3),
            half(count, FIELDS, wide3),
            half(count, FIELDS, wide3),
            full(count, TS, hidden // 2),
            full(rows, 128),
            pltpu.SemaphoreType.DMA((copies,)),
            pltpu.SemaphoreType.DMA((copies,)),
            pltpu.SemaphoreType.DMA((10,)),
        ],
        compiler_params=pltpu.CompilerParams(
            collective_id=0, has_side_effects=True, vmem_limit_bytes=64 * 1024 * 1024
        ),
        cost_estimate=pl.CostEstimate(flops=2_000_000_000, bytes_accessed=4_000_000, transcendentals=200_000),
    )(
        turn_table.T,
        state[0],
        cotangent[0],
        land_sea.reshape(1, CELLS),
        w1[0],
        w2[0],
        w3[0].T,
        gates1[0].T,
        gates2[0].T,
        gates3[0].T,
    )
    results = (up, adj, d1, d2, d3)
    lead = (1, 1, 1, 0, 0)

    def write_all(*refs):
        reads, writes = [], []
        for index in range(5):
            reads.append(pltpu.make_async_copy(refs[index], refs[10 + index], refs[15].at[index]))
            reads[-1].start()
        for index in range(5):
            reads[index].wait()
            target = refs[5 + index].at[0] if lead[index] else refs[5 + index]
            writes.append(pltpu.make_async_copy(refs[10 + index], target, refs[15].at[5 + index]))
            writes[-1].start()
        for copy in writes:
            copy.wait()

    up, adj, d1, d2, d3 = pl.pallas_call(
        write_all,
        out_shape=tuple(
            jax.ShapeDtypeStruct((1,) * extra + value.shape, value.dtype) for extra, value in zip(lead, results)
        ),
        in_specs=[any_space] * 5,
        out_specs=(hbm,) * 5,
        scratch_shapes=[pltpu.VMEM(value.shape, value.dtype) for value in results]
        + [pltpu.SemaphoreType.DMA((10,))],
        compiler_params=pltpu.CompilerParams(vmem_limit_bytes=64 * 1024 * 1024),
    )(*results)
    if rows % 8:
        d3 = d3.T
    return (up, adj, d1, d2.reshape(1, -1)[:, : rows * hidden], d3.reshape(1, -1))


def solution(mesh):
    kernel_spec = P("comp", None, None)
    grid_spec = P("comp", None, "face")
    return jax.shard_map(
        functools.partial(body, mesh.shape["face"]),
        mesh=mesh,
        in_specs=(grid_spec, grid_spec, P("face"), P()) + (kernel_spec,) * 6,
        out_specs=(grid_spec, grid_spec, kernel_spec, P("comp", "face"), P("comp", "face")),
        check_vma=False,
    )
```
